512 devices in a mesh: dp: 32 (over z, core), blk: 16 (over y, x).
Axes of the slice: x: 4, y: 4, z: 16, core: 2. Of those that a mesh axis runs over, the one named last changes fastest.
Arguments:
- partials: bfloat16 [32, 2048, 7168], P('dp', 'blk'), may hold values from -256 to 256
- counts: int32 [32], P('dp'), may hold values from 8 to 32
Outputs:
- update: float32 [2048, 7168], P('blk', 'dp')
The draws below stay inside these ranges and needn't reach their ends.
All inputs are finite; a program needn't handle non-finite values.
Results may differ from the reference program's by a relative error of at most 0.0003.
Values sent between devices are 32-bit elements; how exact they have to be, the bound alone decides.
A program may use at most 64 MiB of HBM per device.

```python
import jax
import jax.numpy as jnp
from jax import lax

H = 2048
D = 7168
ITERS = 3
GROUPS = 32
N_DP = 32


def draw_partials(key, part):
    key = jax.random.fold_in(key, 11)
    keys = jax.random.split(key, 4)
    row_pos = jnp.arange(H, dtype=jnp.float32) / max(H - 1, 1)
    col_pos = jnp.arange(D, dtype=jnp.float32) / max(D - 1, 1)
    row_scale = 10.0 ** jax.random.uniform(keys[0], (H,)) * (1.0 + 2.0 * row_pos)
    col_scale = 10.0 ** jax.random.uniform(keys[1], (D,)) * (1.0 + 2.0 * col_pos)
    paired = jax.random.permutation(keys[2], N_DP)
    block_of = jnp.arange(D) // (D // N_DP)
    spike = jnp.where(block_of[None, :] == paired[:, None], 4.0, 1.0)
    base = jax.random.normal(keys[3], (N_DP, H, D))
    values = 0.02 * base * spike[:, None, :] * row_scale[None, :, None] * col_scale[None, None, :]
    return jnp.clip(values, -256.0, 256.0).astype(jnp.bfloat16)


def set_ends(drawn, rng, least, high):
    place = [jax.random.randint(jax.random.fold_in(rng, axis), (), 0, length) for axis, length in enumerate(drawn.shape)]
    widest = drawn.shape.index(max(drawn.shape))
    neighbour = place[:widest] + [(place[widest] + 1) % drawn.shape[widest]] + place[widest + 1:]
    return drawn.at[tuple(place)].set(least).at[tuple(neighbour)].set(high)


def setup_inputs(seed: int = 0) -> dict:
    key_list = jax.random.split(jax.random.key(seed), 3)
    return {
        "partials": draw_partials(jax.random.fold_in(key_list[2], 71), 0),
        "counts": set_ends(jax.random.randint(key_list[1], (GROUPS,), 8, 33), jax.random.fold_in(key_list[1], 1), 8, 32).astype(jnp.int32),
    }


COEF_A = 3.4445
COEF_B = -4.775
COEF_C = 2.0315
EPS = 1e-07

def mult(left, right):
    return jnp.dot(left, right, precision=lax.Precision.HIGHEST, preferred_element_type=jnp.float32)

def mult_t(left, right):
    return lax.dot_general(left, right, (((1,), (1,)), ((), ())), precision=lax.Precision.HIGHEST, preferred_element_type=jnp.float32)

def reference(partials, counts):

    def add_group(total, pair):
        part, weight = pair
        return (total + part.astype(jnp.float32) * weight.astype(jnp.float32), None)
    grad, _ = lax.scan(add_group, jnp.zeros((H, D), jnp.float32), (partials, counts))
    scale = jnp.sqrt(jnp.sum(grad * grad)) + EPS
    field = grad / scale
    for turn in range(ITERS):
        gram = mult_t(field, field)
        prod = mult(gram, field)
        second = mult(gram, prod)
        field = COEF_A * field + COEF_B * prod + COEF_C * second
    return 0.2 * jnp.sqrt(jnp.float32(max(H, D))) * field
```

```python
import math

import jax
import jax.numpy as jnp
from jax import lax
from jax.experimental import pallas as pl
from jax.experimental.pallas import tpu as pltpu
from jax.sharding import PartitionSpec as P

H = 2048
D = 7168
COEF_A = 3.4445
COEF_B = -4.775
COEF_C = 2.0315
EPS = 1e-07
GAIN = 0.2 * math.sqrt(max(H, D))

Z, CORES, Y, X = 16, 2, 4, 4
NDP, NBLK = Z * CORES, Y * X
ROWS = H // NBLK
COLS = D // NDP
LINE = H // NDP
PACK = LINE + 8
PAIR = 2 * CORES * COLS
MESH = pl.DeviceIdType.MESH
F32 = jnp.float32
BF16 = jnp.bfloat16

G1 = COEF_A * COEF_A
G2 = 2 * COEF_A * COEF_B
G3 = 2 * COEF_A * COEF_C + COEF_B * COEF_B
G4 = 2 * COEF_B * COEF_C
G5 = COEF_C * COEF_C

TREE = {0: (3, 1), 3: (6, 4), 1: (2,), 6: (8, 7), 4: (5,)}


def split(v):
    hi = v.astype(BF16)
    return hi, (v - hi.astype(F32)).astype(BF16)


def mm(left, right):
    m = left.shape[0]
    lh, ll = split(left)
    rh, rl = split(right)
    both = jnp.dot(
        jnp.concatenate([lh, ll], axis=0),
        jnp.concatenate([rh, rl], axis=1),
        preferred_element_type=F32,
    )
    n = right.shape[1]
    return both[:m, :n] + (both[:m, n:] + (both[m:, :n] + both[m:, n:]))


def place():
    d = lax.axis_index("dp")
    b = lax.axis_index("blk")
    return d, b, d // CORES, d % CORES


def up(z, k):
    return lax.rem(z + (k + Z), Z)


def send(src, dst, ssem, rsem, to):
    pltpu.make_async_remote_copy(
        src_ref=src, dst_ref=dst, send_sem=ssem, recv_sem=rsem, device_id=to, device_id_type=MESH
    ).start()


def arrived(ref, sem):
    pltpu.make_async_copy(ref, ref, sem).wait()


def greet():
    d, b, z, c = place()
    bar = pltpu.get_barrier_semaphore()

    def in_plane(i, carry):
        pl.semaphore_signal(bar, inc=1, device_id=(d, lax.rem(b + i, NBLK)), device_id_type=MESH)
        return carry

    lax.fori_loop(1, NBLK, in_plane, 0)
    for k in (1, -1, 2, -2, 3, -3):
        pl.semaphore_signal(bar, inc=1, device_id=(up(z, k) * CORES + c, b), device_id_type=MESH)
    pl.semaphore_signal(bar, inc=1, device_id=(z * CORES + 1 - c, b), device_id_type=MESH)
    pl.semaphore_wait(bar, NBLK - 1 + 7)


class Ring:
    def __init__(self, buf, rows, near, far, cut, sub, sib_send, sib_recv, ring_send, ring_recv):
        self.buf, self.rows, self.near, self.far = buf, rows, near, far
        self.cut, self.sub = cut, sub
        self.sems = sib_send, sib_recv, ring_send, ring_recv
        self.d, self.b, self.z, self.c = place()

    def mine(self, zt, lo, n):
        return self.buf.at[pl.ds(pl.multiple_of((zt * CORES + self.c) * self.rows + lo, 8), n), :]

    def share(self, zt):
        start = pl.multiple_of((zt * CORES + 1 - self.c) * self.rows, 8)
        send(
            self.buf.at[pl.ds(start, self.rows), :],
            self.near.at[zt],
            self.sems[0],
            self.sems[1].at[zt],
            (self.z * CORES + 1 - self.c, self.b),
        )

    def shared(self, zt):
        arrived(self.near.at[zt], self.sems[1].at[zt])

    def pieces(self):
        h = self.rows // self.sub
        return [(q * h, h) for q in range(self.sub)]

    def first(self):
        zt = up(self.z, Z // 2)
        self.shared(zt)
        for q, (lo, n) in enumerate(self.cut):
            side = 0 if q < len(self.cut) // 2 else 1
            part = self.mine(zt, lo, n)
            part[...] = part[...] + self.near[zt, pl.ds(lo, n), :]
            self.push(part, side, 0, q, lo, n)

    def push(self, part, side, step, q, lo, n):
        slot = side * 8 + step
        send(
            part,
            self.far.at[slot, pl.ds(lo, n), :],
            self.sems[2],
            self.sems[3].at[slot * len(self.cut) + q],
            (up(self.z, 1 - 2 * side) * CORES + self.c, self.b),
        )

    def pull(self, side, step, q, lo, n):
        slot = side * 8 + step
        arrived(self.far.at[slot, pl.ds(lo, n), :], self.sems[3].at[slot * len(self.cut) + q])
        return self.far[slot, pl.ds(lo, n), :]

    def second(self):
        for side in (0, 1):
            zt = up(self.z, (1 - 2 * side) * 7)
            self.shared(zt)
        half = len(self.cut) // 2
        for side in (0, 1):
            zt = up(self.z, (1 - 2 * side) * 7)
            for q, (lo, n) in enumerate(self.cut):
                if (q < half) != (side == 0):
                    part = self.mine(zt, lo, n)
                    part[...] = part[...] + self.near[zt, pl.ds(lo, n), :]
                    if self.sub > 1:
                        self.push(part, side, 1, q, lo, n)
        for q, (lo, n) in enumerate(self.cut):
            side = 0 if q < half else 1
            zt = up(self.z, (1 - 2 * side) * 7)
            part = self.mine(zt, lo, n)
            got = self.pull(side, 0, q, lo, n)
            part[...] = part[...] + (self.near[zt, pl.ds(lo, n), :] + got)
            if self.sub > 1:
                self.push(part, side, 1, q, lo, n)
        if self.sub == 1:
            for side in (0, 1):
                zt = up(self.z, (1 - 2 * side) * 7)
                self.push(self.mine(zt, 0, self.rows), side, 1, 0, 0, self.rows)

    def rest(self):
        def step(s, carry):
            for side in (0, 1):
                self.shared(lax.rem(self.z + (1 - 2 * side) * (8 - s) + Z, Z))
            for q, (lo, n) in enumerate(self.pieces()):
                for side in (0, 1):
                    zt = lax.rem(self.z + (1 - 2 * side) * (8 - s) + Z, Z)
                    part = self.mine(zt, lo, n)
                    got = self.pull(side, s - 1, q, lo, n)
                    part[...] = part[...] + (self.near[zt, pl.ds(lo, n), :] + got)
                    self.push(part, side, s, q, lo, n)
            return carry

        lax.fori_loop(2, 8, step, 0)
        self.shared(self.z)

    def total(self, q, lo, n):
        own = self.mine(self.z, lo, n)[...] + self.near[self.z, pl.ds(lo, n), :]
        return own + (self.pull(0, 7, q, lo, n) + self.pull(1, 7, q, lo, n))

    def drain(self):
        arrived(self.near, self.sems[0])
        arrived(self.far.at[pl.ds(0, 15)], self.sems[2])


class Plane:
    def __init__(self, buf, ssem, rsem):
        self.buf, self.ssem, self.rsem = buf, ssem, rsem
        self.d, self.b, _, _ = place()

    def start(self, value):
        mine = self.buf.at[:, pl.ds(pl.multiple_of(self.b * 128, 128), 128)]
        mine[...] = value

        def one(i, carry):
            send(mine, mine, self.ssem, self.rsem, (self.d, lax.rem(self.b + i, NBLK)))
            return carry

        lax.fori_loop(1, NBLK, one, 0)

    def finish(self):
        arrived(self.buf.at[:, pl.ds(0, (NBLK - 1) * 128)], self.rsem)

    def drain(self):
        arrived(self.buf.at[:, pl.ds(0, (NBLK - 1) * 128)], self.ssem)


class Line:
    def __init__(self, buf, ssem, rsem, share_ssem, share_rsem):
        self.buf, self.ssem, self.rsem = buf, ssem, rsem
        self.share_sems = share_ssem, share_rsem
        self.d, self.b, self.z, self.c = place()

    def part(self, side, k, child):
        dd = up(self.z, -side * k) * CORES + self.c
        lo, n = 0, LINE
        if child == 8:
            n = LINE // 2
            lo = 0 if side > 0 else n
        return self.buf.at[pl.ds(pl.multiple_of(dd * LINE + lo, 8), n), :]

    def sem(self, side, k):
        return self.rsem.at[(0 if side > 0 else 8) + k - 1]

    def emit(self, k):
        for child in TREE.get(k, ()):
            for side in (1, -1):
                v = self.part(side, k, child)
                to = up(self.z, side * (child - k)) * CORES + self.c
                send(v, v, self.ssem, self.sem(side, child), (to, self.b))

    def share(self, dz):
        dd = up(self.z, dz) * CORES + self.c
        v = self.buf.at[pl.ds(pl.multiple_of(dd * LINE, 8), LINE), :]
        send(v, v, self.share_sems[0], self.share_sems[1], (self.z * CORES + 1 - self.c, self.b))

    def start(self, value):
        v = self.buf.at[pl.ds(pl.multiple_of(self.d * LINE, 8), LINE), :]
        v[...] = value
        self.emit(0)
        self.share(0)

    def take(self, k):
        for side in (1, -1):
            arrived(self.part(side, k, k), self.sem(side, k))
        self.emit(k)
        self.share(-k)
        if k != 8:
            self.share(k)

    def relay(self, stage):
        for k in ((3, 1), (6, 4, 2), (5, 7, 8))[stage]:
            self.take(k)

    def finish(self):
        arrived(self.buf.at[pl.ds(0, H // 2), :], self.share_sems[1])

    def drain(self):
        arrived(self.buf.at[pl.ds(0, 15 * LINE), :], self.ssem)
        arrived(self.buf.at[pl.ds(0, H // 2), :], self.share_sems[0])


def eye(rows, cols, row0, col0, value):
    r = lax.broadcasted_iota(jnp.int32, (rows, cols), 0) + row0
    c = lax.broadcasted_iota(jnp.int32, (rows, cols), 1) + col0
    return jnp.where(r == c, F32(value), F32(0))


def kernel(
    counts, partials, out, pt, sb, rv, ft, pg, sg, rg, zb, xb, yt,
    sib_s, sib_r, ring_s, ring_r, gsib_s, gsib_r, gring_s, gring_r,
    plane_s, plane_r, line_s, line_r, lshare_s, lshare_r,
):
    d, b, z, c = place()
    greet()

    weight = counts[0].astype(F32)
    scaled_eye = (eye(128, 128, 0, 0, 1.0) * weight).astype(BF16)
    ring = Ring(
        pt, COLS, sb, rv, [(q * 56, 56) for q in range(4)], 4, sib_s, sib_r, ring_s, ring_r
    )
    pair0 = up(z, Z // 2) // 2

    def turn(j):
        pair = lax.rem(pair0 + j + 8, 8)
        for t in range(7):
            at = pl.multiple_of(pair * PAIR + t * 128, 128)
            tile = partials[0, :, pl.ds(at, 128)]
            pt[pl.ds(at, 128), :] = lax.dot_general(
                scaled_eye, tile, (((1,), (1,)), ((), ())), preferred_element_type=F32
            )
        ring.share(pair * 2)
        ring.share(pair * 2 + 1)

    for j in (0, -1, 1):
        turn(j)
    ring.first()
    for j in (-2, 2, -3, 3, 4):
        turn(j)
    ring.second()
    ring.rest()
    field = jnp.concatenate([ring.total(q, q * 56, 56) for q in range(4)], axis=0)

    whole = Plane(ft, plane_s.at[7], plane_r.at[7])
    whole.start(field)
    whole.finish()

    fh, fl = split(ft[:, pl.ds(pl.multiple_of(b * 128, 128), 128)])
    right = jnp.concatenate([fh, fl], axis=1)

    def gram(i, sq):
        v = ft[:, pl.ds(pl.multiple_of(i * 128, 128), 128)]
        vh, vl = split(v)
        both = lax.dot_general(
            jnp.concatenate([vh, vl], axis=1), right, (((0,), (0,)), ((), ())), preferred_element_type=F32
        )
        res = both[:128, :128] + (both[:128, 128:] + (both[128:, :128] + both[128:, 128:]))
        at = pl.multiple_of(i * 2 * PACK, 8)
        pg[pl.ds(at, LINE), :] = res[:LINE]
        pg[pl.ds(pl.multiple_of(at + PACK, 8), LINE), :] = res[LINE:]
        return sq + jnp.sum(v * v, axis=0, keepdims=True)

    sq = lax.fori_loop(0, NBLK, gram, jnp.zeros((1, 128), F32))
    sq = jnp.broadcast_to(jnp.sum(sq, axis=1, keepdims=True), (8, 128))

    def put(i, carry):
        pg[pl.ds(pl.multiple_of(i * PACK + LINE, 8), 8), :] = sq
        return carry

    lax.fori_loop(0, NDP, put, 0)

    gr = Ring(pg, PACK, sg, rg, [(0, 40), (40, 32)], 1, gsib_s, gsib_r, gring_s, gring_r)

    def share(i, carry):
        gr.share(lax.rem(z + 8 + i, Z))
        return carry

    lax.fori_loop(0, Z, share, 0)
    gr.first()
    gr.second()
    gr.rest()
    packed = gr.total(0, 0, PACK)
    scale = jnp.sqrt(packed[LINE:LINE + 1, :]) + EPS
    inv = 1.0 / scale
    g = packed[:LINE] * (inv * inv)

    def line(i):
        return Line(zb.at[i], line_s.at[i], line_r.at[i], lshare_s.at[i], lshare_r.at[i])

    def plane(i):
        return Plane(xb.at[i], plane_s.at[i], plane_r.at[i])

    used = []

    def turn_field(g, base, between):
        zg, zs = line(base), line(base + 1)
        xg, xs, xw = plane(base * 3 // 2), plane(base * 3 // 2 + 1), plane(base * 3 // 2 + 2)
        used.extend([zg, zs, xg, xs, xw])
        zg.start(g)
        xg.start(g)
        for stage in range(3):
            zg.relay(stage)
        xg.finish()
        zg.finish()
        s = mm(xg.buf[...], zg.buf[...])
        zs.start(s)
        xs.start(s)
        zs.relay(0)
        xs.finish()
        t = mm(xs.buf[...], zg.buf[...])
        w = G3 * g + G4 * s + G5 * t
        xw.start(w)
        zs.relay(1)
        between(xg.buf, xs.buf)
        zs.relay(2)
        zs.finish()
        xw.finish()
        return G1 * g + G2 * s + mm(xw.buf[...], zs.buf[...])

    g = turn_field(g, 0, lambda xg, xs: None)

    zq = line(6)
    used.append(zq)

    def between(xg, xs):
        left = COEF_B * xg[...] + COEF_C * xs[...] + eye(LINE, H, d * LINE, 0, COEF_A)
        right = COEF_B * zb[0] + COEF_C * zb[1] + eye(H, 128, 0, b * 128, COEF_A)
        zq.start(mm(left, right))

    g = turn_field(g, 2, between)

    zg, zs = line(4), line(5)
    xg = plane(6)
    xy = Plane(yt, plane_s.at[8], plane_r.at[8])
    used.extend([zg, zs, xg, xy, whole, ring, gr])
    zq.relay(0)
    zg.start(g)
    xg.start(g)
    zq.relay(1)
    zg.relay(0)
    zq.relay(2)
    zq.finish()
    xy.start(mm(ft[...], zb[6]) * (inv * GAIN))
    zg.relay(1)
    zg.relay(2)
    xg.finish()
    zg.finish()
    zs.start(mm(xg.buf[...], zg.buf[...]))
    for stage in range(3):
        zs.relay(stage)
    zs.finish()
    xy.finish()
    last = COEF_B * zg.buf[...] + COEF_C * zs.buf[...] + eye(H, 128, 0, b * 128, COEF_A)
    out[...] = mm(yt[...], last)
    for one in used:
        one.drain()


def body(partials, counts):
    vmem = pltpu.VMEM
    dma = pltpu.SemaphoreType.DMA
    out = pl.pallas_call(
        kernel,
        name="newton_schulz",
        out_shape=jax.ShapeDtypeStruct((COLS, ROWS), F32),
        in_specs=[
            pl.BlockSpec(memory_space=pltpu.SMEM),
            pl.BlockSpec(memory_space=pltpu.VMEM),
        ],
        out_specs=pl.BlockSpec(memory_space=pltpu.VMEM),
        scratch_shapes=[
            vmem((D, 128), F32),
            vmem((Z, COLS, 128), F32),
            vmem((16, COLS, 128), F32),
            vmem((COLS, H), F32),
            vmem((NDP * PACK, 128), F32),
            vmem((Z, PACK, 128), F32),
            vmem((16, PACK, 128), F32),
            vmem((7, H, 128), F32),
            vmem((7, LINE, H), F32),
            vmem((COLS, H), F32),
            dma, dma((Z,)), dma, dma((64,)),
            dma, dma((Z,)), dma, dma((32,)),
            dma((9,)), dma((9,)),
            dma((7,)), dma((7, 16)), dma((7,)), dma((7,)),
        ],
        compiler_params=pltpu.CompilerParams(
            collective_id=0, has_side_effects=True, vmem_limit_bytes=56 * 2**20
        ),
    )(counts, partials)
    return out.T


def solution(mesh):
    placed = (P("dp", "blk", None), P("dp"))
    return jax.shard_map(
        body, mesh=mesh, in_specs=placed, out_specs=P("blk", "dp"), check_vma=False
    )
```

```python
import math

import jax
import jax.numpy as jnp
from jax import lax
from jax.experimental import pallas as pl
from jax.experimental.pallas import tpu as pltpu
from jax.sharding import PartitionSpec as P

H = 2048
D = 7168
COEF_A = 3.4445
COEF_B = -4.775
COEF_C = 2.0315
EPS = 1e-07
GAIN = 0.2 * math.sqrt(max(H, D))

Z, CORES, Y, X = 16, 2, 4, 4
NDP, NBLK = Z * CORES, Y * X
ROWS = H // NBLK
COLS = D // NDP
LINE = H // NDP
PACK = LINE + 8
HALF = 40
PAIR = 2 * CORES * COLS
MESH = pl.DeviceIdType.MESH
F32 = jnp.float32
BF16 = jnp.bfloat16

TREE = {0: (3, 1), 3: (6, 4), 1: (2,), 6: (8, 7), 4: (5,)}
PARENT = {child: k for k, children in TREE.items() for child in children}


def split(v):
    hi = v.astype(BF16)
    return hi, (v - hi.astype(F32)).astype(BF16)


def cut(right, halves):
    hi, lo = split(right)
    halves[:, :128] = hi
    halves[:, 128:] = lo


def mm(left, halves):
    m = left.shape[0]
    lh, ll = split(left)
    both = jnp.dot(jnp.concatenate([lh, ll], axis=0), halves[...], preferred_element_type=F32)
    return both[:m, :128] + (both[:m, 128:] + (both[m:, :128] + both[m:, 128:]))


def place():
    d = lax.axis_index("dp")
    b = lax.axis_index("blk")
    return d, b, d // CORES, d % CORES


def up(z, k):
    return lax.rem(z + (k + Z), Z)


def send(src, dst, ssem, rsem, to):
    pltpu.make_async_remote_copy(
        src_ref=src, dst_ref=dst, send_sem=ssem, recv_sem=rsem, device_id=to, device_id_type=MESH
    ).start()


def arrived(ref, sem):
    pltpu.make_async_copy(ref, ref, sem).wait()


def greet():
    d, b, z, c = place()
    bar = pltpu.get_barrier_semaphore()

    def in_plane(i, carry):
        pl.semaphore_signal(bar, inc=1, device_id=(d, lax.rem(b + i, NBLK)), device_id_type=MESH)
        return carry

    lax.fori_loop(1, NBLK, in_plane, 0)
    for k in (1, -1, 2, -2, 3, -3):
        pl.semaphore_signal(bar, inc=1, device_id=(up(z, k) * CORES + c, b), device_id_type=MESH)
    pl.semaphore_signal(bar, inc=1, device_id=(z * CORES + 1 - c, b), device_id_type=MESH)


def met():
    pl.semaphore_wait(pltpu.get_barrier_semaphore(), NBLK - 1 + 7)


class Ring:
    def __init__(self, buf, rows, near, far, cut, sub, sib_send, sib_recv, ring_send, ring_recv):
        self.buf, self.rows, self.near, self.far = buf, rows, near, far
        self.cut, self.sub = cut, sub
        self.sems = sib_send, sib_recv, ring_send, ring_recv
        self.d, self.b, self.z, self.c = place()

    def mine(self, zt, lo, n):
        return self.buf.at[pl.ds(pl.multiple_of((zt * CORES + self.c) * self.rows + lo, 8), n), :]

    def share(self, zt):
        start = pl.multiple_of((zt * CORES + 1 - self.c) * self.rows, 8)
        send(
            self.buf.at[pl.ds(start, self.rows), :],
            self.near.at[zt],
            self.sems[0],
            self.sems[1].at[zt],
            (self.z * CORES + 1 - self.c, self.b),
        )

    def shared(self, zt):
        arrived(self.near.at[zt], self.sems[1].at[zt])

    def pieces(self):
        h = self.rows // self.sub
        return [(q * h, h) for q in range(self.sub)]

    def first(self):
        zt = up(self.z, Z // 2)
        self.shared(zt)
        for q, (lo, n) in enumerate(self.cut):
            side = 0 if q < len(self.cut) // 2 else 1
            part = self.mine(zt, lo, n)
            part[...] = part[...] + self.near[zt, pl.ds(lo, n), :]
            self.push(part, side, 0, q, lo, n)

    def push(self, part, side, step, q, lo, n):
        slot = side * 8 + step
        send(
            part,
            self.far.at[slot, pl.ds(lo, n), :],
            self.sems[2],
            self.sems[3].at[slot * len(self.cut) + q],
            (up(self.z, 1 - 2 * side) * CORES + self.c, self.b),
        )

    def pull(self, side, step, q, lo, n):
        slot = side * 8 + step
        arrived(self.far.at[slot, pl.ds(lo, n), :], self.sems[3].at[slot * len(self.cut) + q])
        return self.far[slot, pl.ds(lo, n), :]

    def second(self):
        for side in (0, 1):
            zt = up(self.z, (1 - 2 * side) * 7)
            self.shared(zt)
        half = len(self.cut) // 2
        for side in (0, 1):
            zt = up(self.z, (1 - 2 * side) * 7)
            for q, (lo, n) in enumerate(self.cut):
                if (q < half) != (side == 0):
                    part = self.mine(zt, lo, n)
                    part[...] = part[...] + self.near[zt, pl.ds(lo, n), :]
                    if self.sub > 1:
                        self.push(part, side, 1, q, lo, n)
        for q, (lo, n) in enumerate(self.cut):
            side = 0 if q < half else 1
            zt = up(self.z, (1 - 2 * side) * 7)
            part = self.mine(zt, lo, n)
            got = self.pull(side, 0, q, lo, n)
            part[...] = part[...] + (self.near[zt, pl.ds(lo, n), :] + got)
            if self.sub > 1:
                self.push(part, side, 1, q, lo, n)
        if self.sub == 1:
            for side in (0, 1):
                zt = up(self.z, (1 - 2 * side) * 7)
                self.push(self.mine(zt, 0, self.rows), side, 1, 0, 0, self.rows)

    def rest(self):
        def step(s, carry):
            for side in (0, 1):
                self.shared(lax.rem(self.z + (1 - 2 * side) * (8 - s) + Z, Z))
            for q, (lo, n) in enumerate(self.pieces()):
                for side in (0, 1):
                    zt = lax.rem(self.z + (1 - 2 * side) * (8 - s) + Z, Z)
                    part = self.mine(zt, lo, n)
                    got = self.pull(side, s - 1, q, lo, n)
                    part[...] = part[...] + (self.near[zt, pl.ds(lo, n), :] + got)
                    self.push(part, side, s, q, lo, n)
            return carry

        lax.fori_loop(2, 8, step, 0)
        self.shared(self.z)

    def total(self, q, lo, n):
        own = self.mine(self.z, lo, n)[...] + self.near[self.z, pl.ds(lo, n), :]
        return own + (self.pull(0, 7, q, lo, n) + self.pull(1, 7, q, lo, n))

    def drain(self):
        arrived(self.near, self.sems[0])
        arrived(self.far.at[pl.ds(0, 15)], self.sems[2])


class Fold:
    def __init__(self, buf, near, far, sib_send, sib_recv, ssem, rsem):
        self.buf, self.near, self.far = buf, near, far
        self.sems = sib_send, sib_recv, ssem, rsem
        self.d, self.b, self.z, self.c = place()

    def share(self, zt):
        start = pl.multiple_of((zt * CORES + 1 - self.c) * PACK, 8)
        send(
            self.buf.at[pl.ds(start, PACK), :],
            self.near.at[zt],
            self.sems[0],
            self.sems[1].at[zt],
            (self.z * CORES + 1 - self.c, self.b),
        )

    def span(self, side, k):
        if k != 8:
            return 0, PACK
        return (0, HALF) if side > 0 else (HALF, PACK - HALF)

    def landing(self, side, k):
        slot = (0 if side > 0 else 8) + k - 1
        lo, n = self.span(side, k)
        return self.far.at[slot, pl.ds(lo, n), :], self.sems[3].at[slot]

    def collect(self, zt, takes):
        arrived(self.near.at[zt], self.sems[1].at[zt])
        part = self.buf.at[pl.ds(pl.multiple_of((zt * CORES + self.c) * PACK, 8), PACK), :]
        part[...] = part[...] + self.near[zt]
        for side, child in takes:
            ref, sem = self.landing(side, child)
            lo, n = self.span(side, child)
            arrived(ref, sem)
            rows = part.at[pl.ds(lo, n), :]
            rows[...] = rows[...] + ref[...]
        return part

    def push(self, part, side, k):
        ref, sem = self.landing(side, k)
        lo, n = self.span(side, k)
        to = up(self.z, side * (k - PARENT[k])) * CORES + self.c
        send(part.at[pl.ds(lo, n), :], ref, self.sems[2], sem, (to, self.b))

    def run(self):
        part = self.collect(up(self.z, 8), ())
        for side in (1, -1):
            self.push(part, side, 8)
        for k in (7, 5, 2, 6, 4, 1, 3):
            for side in (1, -1):
                part = self.collect(up(self.z, side * k), [(side, n) for n in TREE.get(k, ())])
                self.push(part, side, k)
        return self.collect(self.z, [(side, n) for n in TREE[0] for side in (1, -1)])[...]

    def drain(self):
        arrived(self.near, self.sems[0])
        arrived(self.far.at[pl.ds(0, 15)], self.sems[2])


class Spread:
    def __init__(self, buf, ssem, rsem):
        self.buf, self.ssem, self.rsem = buf, ssem, rsem
        self.d, self.b, _, self.c = place()

    def block(self, u, v):
        y, x = self.b // X, self.b % X
        first = self.c == 0
        xx = lax.rem(x + jnp.where(first, u, v) + X, X)
        yy = lax.rem(y + jnp.where(first, v, u) + Y, Y)
        return yy * X + xx

    def part(self, u, v, half):
        lo, n = {0: (0, COLS), 1: (0, COLS // 2), 2: (COLS // 2, COLS // 2)}[half]
        return self.buf.at[pl.ds(lo, n), pl.ds(pl.multiple_of(self.block(u, v) * 128, 128), 128)]

    def sem(self, u, v, half):
        return self.rsem.at[((u + 1) * 4 + v + 1) * 2 + half // 2]

    def send(self, u, v, half, axis, step):
        to = (step, 0) if axis == 0 else (0, step)
        seen = [u - to[0], v - to[1]]
        seen = [2 if n == -2 else n for n in seen]
        ref = self.part(u, v, half)
        send(ref, ref, self.ssem, self.sem(*seen, half), (self.d, self.block(*to)))

    def take(self, u, v, half=0):
        arrived(self.part(u, v, half), self.sem(u, v, half))

    def steps(self, value):
        self.part(0, 0, 0)[...] = value
        for axis in (0, 1):
            for step in (1, -1):
                self.send(0, 0, 0, axis, step)
        yield [self.b]
        for u, half in ((-1, 1), (1, 2)):
            self.take(u, 0)
            self.send(u, 0, half, 0, -u)
            for step in (1, -1):
                self.send(u, 0, 0, 1, step)
        for v, half in ((-1, 1), (1, 2)):
            self.take(0, v)
            self.send(0, v, half, 1, -v)
        yield [self.block(-1, 0), self.block(1, 0)]
        for half in (1, 2):
            self.take(2, 0, half)
        for step in (1, -1):
            self.send(2, 0, 0, 1, step)
        yield [self.block(0, -1), self.block(0, 1), self.block(2, 0)]
        for u in (-1, 1, 2):
            for v, half in ((-1, 1), (1, 2)):
                self.take(u, v)
                self.send(u, v, half, 1, -v)
            yield [self.block(u, -1), self.block(u, 1)]
        for u in (0, -1, 1, 2):
            for half in (1, 2):
                self.take(u, 2, half)
            yield [self.block(u, 2)]

    def drain(self):
        arrived(self.buf.at[:, pl.ds(0, (NBLK - 1) * 128)], self.ssem)


class Plane:
    def __init__(self, buf, ssem, rsem):
        self.buf, self.ssem, self.rsem = buf, ssem, rsem
        self.d, self.b, _, _ = place()

    def start(self, value):
        mine = self.buf.at[:, pl.ds(pl.multiple_of(self.b * 128, 128), 128)]
        mine[...] = value

        def one(i, carry):
            send(mine, mine, self.ssem, self.rsem, (self.d, lax.rem(self.b + i, NBLK)))
            return carry

        lax.fori_loop(1, NBLK, one, 0)

    def finish(self):
        arrived(self.buf.at[:, pl.ds(0, (NBLK - 1) * 128)], self.rsem)

    def drain(self):
        arrived(self.buf.at[:, pl.ds(0, (NBLK - 1) * 128)], self.ssem)


class Line:
    def __init__(self, buf, ssem, rsem, share_ssem, share_rsem):
        self.buf, self.ssem, self.rsem = buf, ssem, rsem
        self.share_sems = share_ssem, share_rsem
        self.d, self.b, self.z, self.c = place()

    def part(self, side, k, child):
        dd = up(self.z, -side * k) * CORES + self.c
        lo, n = 0, LINE
        if child == 8:
            n = LINE // 2
            lo = 0 if side > 0 else n
        return self.buf.at[pl.ds(pl.multiple_of(dd * LINE + lo, 8), n), :]

    def sem(self, side, k):
        return self.rsem.at[(0 if side > 0 else 8) + k - 1]

    def emit(self, k):
        for child in TREE.get(k, ()):
            for side in (1, -1):
                v = self.part(side, k, child)
                to = up(self.z, side * (child - k)) * CORES + self.c
                send(v, v, self.ssem, self.sem(side, child), (to, self.b))

    def share(self, dz):
        dd = up(self.z, dz) * CORES + self.c
        v = self.buf.at[pl.ds(pl.multiple_of(dd * LINE, 8), LINE), :]
        send(v, v, self.share_sems[0], self.share_sems[1], (self.z * CORES + 1 - self.c, self.b))

    def start(self, value):
        v = self.buf.at[pl.ds(pl.multiple_of(self.d * LINE, 8), LINE), :]
        v[...] = value
        self.emit(0)
        self.share(0)

    def take(self, k):
        for side in (1, -1):
            arrived(self.part(side, k, k), self.sem(side, k))
        self.emit(k)
        self.share(-k)
        if k != 8:
            self.share(k)

    def relay(self, stage):
        for k in ((3, 1), (6, 4, 2), (5, 7, 8))[stage]:
            self.take(k)

    def finish(self):
        arrived(self.buf.at[pl.ds(0, H // 2), :], self.share_sems[1])

    def drain(self):
        arrived(self.buf.at[pl.ds(0, 15 * LINE), :], self.ssem)
        arrived(self.buf.at[pl.ds(0, H // 2), :], self.share_sems[0])


def eye(rows, cols, row0, col0, value):
    r = lax.broadcasted_iota(jnp.int32, (rows, cols), 0) + row0
    c = lax.broadcasted_iota(jnp.int32, (rows, cols), 1) + col0
    return jnp.where(r == c, F32(value), F32(0))


def kernel(
    counts, partials, out, pin, pt, sb, rv, ft, pg, sg, rg, zb, xb, xg0, yt, zc, zd,
    in_s, sib_s, sib_r, ring_s, ring_r, field_s, field_r, gsib_s, gsib_r, fold_s, fold_r,
    plane_s, plane_r, line_s, line_r, lshare_s, lshare_r,
):
    d, b, z, c = place()
    greet()
    pair0 = up(z, Z // 2) // 2

    def load(j):
        at = pl.multiple_of(lax.rem(pair0 + j + 8, 8) * PAIR, 128)
        window = pl.ds(at, PAIR)
        return pltpu.make_async_copy(partials.at[0, :, window], pin.at[:, window], in_s.at[j + 3])

    turns = (0, -1, 1, -2, 2, -3, 3, 4)
    for j in turns:
        load(j).start()

    weight = counts[0].astype(F32)
    scaled_eye = (eye(128, 128, 0, 0, 1.0) * weight).astype(BF16)
    for j in turns:
        load(j).wait()
        pair = lax.rem(pair0 + j + 8, 8)
        for t in range(7):
            at = pl.multiple_of(pair * PAIR + t * 128, 128)
            pt[pl.ds(at, 128), :] = lax.dot_general(
                scaled_eye, pin[:, pl.ds(at, 128)], (((1,), (1,)), ((), ())), preferred_element_type=F32
            )
    met()
    used = []
    ring = Ring(
        pt, COLS, sb, rv, [(q * 32, 32) for q in range(7)], 7, sib_s, sib_r, ring_s, ring_r
    )
    used.append(ring)
    for j in turns:
        pair = lax.rem(pair0 + j + 8, 8)
        ring.share(pair * 2)
        ring.share(pair * 2 + 1)
    ring.first()
    ring.second()
    ring.rest()
    field = jnp.concatenate([ring.total(q, lo, n) for q, (lo, n) in enumerate(ring.cut)], axis=0)

    sq = jnp.sum(jnp.sum(field * field, axis=0, keepdims=True), axis=1, keepdims=True)
    sq = jnp.broadcast_to(sq, (8, 128))

    def put(i, carry):
        pg[pl.ds(pl.multiple_of(i * PACK + LINE, 8), 8), :] = sq
        return carry

    fold = Fold(pg, sg, rg, gsib_s, gsib_r, fold_s, fold_r)
    whole = Spread(ft, field_s.at[0], field_r.at[0])
    used.extend([whole, fold])
    right = jnp.concatenate(split(field), axis=1)

    def gram(i):
        v = jnp.concatenate(split(ft[:, pl.ds(pl.multiple_of(i * 128, 128), 128)]), axis=1)
        both = lax.dot_general(v, right, (((0,), (0,)), ((), ())), preferred_element_type=F32)
        res = both[:128, :128] + (both[:128, 128:] + (both[128:, :128] + both[128:, 128:]))
        at = pl.multiple_of(i * 2 * PACK, 8)
        pg[pl.ds(at, LINE), :] = res[:LINE]
        pg[pl.ds(pl.multiple_of(at + PACK, 8), LINE), :] = res[LINE:]
        fold.share(i)

    lax.fori_loop(0, NDP, put, 0)
    for blocks in whole.steps(field):
        for i in blocks:
            gram(i)
    packed = fold.run()

    def line(i):
        one = Line(zb.at[i], line_s.at[i], line_r.at[i], lshare_s.at[i], lshare_r.at[i])
        used.append(one)
        return one

    def plane(i, buf):
        one = Plane(buf, plane_s.at[i], plane_r.at[i])
        used.append(one)
        return one

    def square(packed, zg, xg, beside=lambda stage: None):
        zg.start(packed[:LINE])
        xg.start(packed)
        beside(0)
        for stage in range(3):
            zg.relay(stage)
            beside(stage + 1)
        xg.finish()
        inv = F32(1)
        if packed.shape[0] > LINE:
            tiles = xg.buf[LINE:LINE + 1, :]
            total = sum(tiles[:, i * 128:(i + 1) * 128] for i in range(NBLK))
            inv = 1.0 / (jnp.sqrt(total[0, 0]) + EPS)
        left = xg.buf[:LINE, :] * (inv * inv)
        zg.finish()
        cut(zg.buf[...], zc)
        g = packed[:LINE] * (inv * inv)
        return inv, COEF_B * g + COEF_C * (mm(left, zc) * (inv * inv)) + eye(LINE, 128, d * LINE, b * 128, COEF_A)

    def advance(packed, i, beside=lambda stage: None):
        zg = line(2 * i)
        inv, p = square(packed, zg, plane(3 * i, xg0 if i == 0 else xb.at[0]), beside)
        zp, xp, xu = line(2 * i + 1), plane(3 * i + 1, xb.at[1 + 2 * i]), plane(3 * i + 2, xb.at[2 + 2 * i])
        zp.start(p)
        xp.start(p)
        beside(4)
        zp.relay(0)
        xp.finish()
        xu.start(mm(xp.buf[...], zc) * (inv * inv))
        zp.relay(1)
        zp.relay(2)
        zp.finish()
        cut(zp.buf[...], zd)
        xu.finish()
        return inv, mm(xu.buf[...], zd)

    inv, g = advance(packed, 0)

    def apply(i, value):
        one = Spread(yt.at[i], field_s.at[i + 1], field_r.at[i + 1])
        used.append(one)
        moves = []

        def beside(stage):
            if stage == 0:
                moves.append(one.steps(value()))
            for _ in range((1, 1, 2, 2, 9)[stage]):
                next(moves[0], None)

        return beside

    first = apply(0, lambda: mm(ft[...], zd))
    _, g = advance(g, 1, first)
    second = apply(1, lambda: mm(yt[0], zd) * (inv * GAIN))
    _, p = square(g, line(4), plane(6, xb.at[5]), second)
    zp = line(5)
    zp.start(p)
    second(4)
    for stage in range(3):
        zp.relay(stage)
    zp.finish()
    cut(zp.buf[...], zd)
    out[...] = mm(yt[1], zd)
    for one in used:
        one.drain()


def body(partials, counts):
    vmem = pltpu.VMEM
    dma = pltpu.SemaphoreType.DMA
    out = pl.pallas_call(
        kernel,
        name="newton_schulz",
        out_shape=jax.ShapeDtypeStruct((COLS, ROWS), F32),
        in_specs=[
            pl.BlockSpec(memory_space=pltpu.SMEM),
            pl.BlockSpec(memory_space=pl.ANY),
        ],
        out_specs=pl.BlockSpec(memory_space=pltpu.VMEM),
        scratch_shapes=[
            vmem((ROWS, D), BF16),
            vmem((D, 128), F32),
            vmem((Z, COLS, 128), F32),
            vmem((16, COLS, 128), F32),
            vmem((COLS, H), F32),
            vmem((NDP * PACK, 128), F32),
            vmem((Z, PACK, 128), F32),
            vmem((16, PACK, 128), F32),
            vmem((6, H, 128), F32),
            vmem((6, LINE, H), F32),
            vmem((PACK, H), F32),
            vmem((2, COLS, H), F32),
            vmem((H, 256), BF16),
            vmem((H, 256), BF16),
            dma((8,)), dma, dma((Z,)), dma, dma((112,)),
            dma((3,)), dma((3, 32)),
            dma, dma((Z,)), dma, dma((16,)),
            dma((7,)), dma((7,)),
            dma((6,)), dma((6, 16)), dma((6,)), dma((6,)),
        ],
        compiler_params=pltpu.CompilerParams(
            collective_id=0, has_side_effects=True, vmem_limit_bytes=56 * 2**20
        ),
    )(counts, partials)
    return out.T


def solution(mesh):
    placed = (P("dp", "blk", None), P("dp"))
    return jax.shard_map(
        body, mesh=mesh, in_specs=placed, out_specs=P("blk", "dp"), check_vma=False
    )
```

```python
import math

import jax
import jax.numpy as jnp
from jax import lax
from jax.experimental import pallas as pl
from jax.experimental.pallas import tpu as pltpu
from jax.sharding import PartitionSpec as P

H = 2048
D = 7168
COEF_A = 3.4445
COEF_B = -4.775
COEF_C = 2.0315
EPS = 1e-07
GAIN = 0.2 * math.sqrt(max(H, D))

Z, CORES, Y, X = 16, 2, 4, 4
NDP, NBLK = Z * CORES, Y * X
ROWS = H // NBLK
COLS = D // NDP
LINE = H // NDP
PACK = LINE + 8
CUT = 128
HALF = 40
PAIR = 2 * CORES * COLS
MESH = pl.DeviceIdType.MESH
F32 = jnp.float32
BF16 = jnp.bfloat16

TREE = {0: (3, 1), 3: (6, 4), 1: (2,), 6: (8, 7), 4: (5,)}
RELAY = {0: (5, 2, 1), 5: (8, 7, 6, 4), 2: (3,)}
STAGES = ((2, 1, 5), (4, 6), (3, 7, 8))
SETS = (((2, -2), (1, -1), (5, -5)), ((4, -4), (6, -6)), ((3, -3), (7, -7), (8, 0)))
PARENT = {child: k for k, children in TREE.items() for child in children}
NEAR = sorted(((u, v) for u in (-1, 0, 1, 2) for v in (-1, 0, 1, 2)), key=lambda o: abs(o[0]) + abs(o[1]))
PARENT = {child: k for k, children in TREE.items() for child in children}


def split(v):
    hi = v.astype(BF16)
    return hi, (v - hi.astype(F32)).astype(BF16)


def stack(v, axis):
    return jnp.concatenate(split(v), axis=axis)


def merge(both):
    m = both.shape[0] // 2
    return both[:m, :128] + (both[:m, 128:] + (both[m:, :128] + both[m:, 128:]))


def flat(buf):
    return jnp.concatenate([buf[i] for i in range(NBLK)], axis=1)


def dot(left, right):
    return jnp.dot(left, right, preferred_element_type=F32)


def mm(left, halves):
    return merge(dot(stack(left, 0), halves[...]))


def place():
    d = lax.axis_index("dp")
    b = lax.axis_index("blk")
    return d, b, d // CORES, d % CORES


def up(z, k):
    return lax.rem(z + (k + Z), Z)


def up4(i, k):
    return lax.rem(i + (k + 4), 4)


def send(src, dst, ssem, rsem, to):
    pltpu.make_async_remote_copy(
        src_ref=src, dst_ref=dst, send_sem=ssem, recv_sem=rsem, device_id=to, device_id_type=MESH
    ).start()


def arrived(ref, sem):
    pltpu.make_async_copy(ref, ref, sem).wait()


def greet():
    d, b, z, c = place()
    bar = pltpu.get_barrier_semaphore()

    def in_plane(i, carry):
        pl.semaphore_signal(bar, inc=1, device_id=(d, lax.rem(b + i, NBLK)), device_id_type=MESH)
        return carry

    lax.fori_loop(1, NBLK, in_plane, 0)
    for k in (1, -1, 2, -2, 3, -3, 5, -5):
        pl.semaphore_signal(bar, inc=1, device_id=(up(z, k) * CORES + c, b), device_id_type=MESH)
    pl.semaphore_signal(bar, inc=1, device_id=(z * CORES + 1 - c, b), device_id_type=MESH)


def met():
    pl.semaphore_wait(pltpu.get_barrier_semaphore(), NBLK - 1 + 9)


class Ring:
    def __init__(self, buf, rows, near, far, cut, sub, sib_send, sib_recv, ring_send, ring_recv):
        self.buf, self.rows, self.near, self.far = buf, rows, near, far
        self.cut, self.sub = cut, sub
        self.sems = sib_send, sib_recv, ring_send, ring_recv
        self.d, self.b, self.z, self.c = place()

    def mine(self, zt, lo, n):
        return self.buf.at[pl.ds(pl.multiple_of((zt * CORES + self.c) * self.rows + lo, 8), n), :]

    def share(self, zt):
        start = pl.multiple_of((zt * CORES + 1 - self.c) * self.rows, 8)
        send(
            self.buf.at[pl.ds(start, self.rows), :],
            self.near.at[zt],
            self.sems[0],
            self.sems[1].at[zt],
            (self.z * CORES + 1 - self.c, self.b),
        )

    def shared(self, zt):
        arrived(self.near.at[zt], self.sems[1].at[zt])

    def pieces(self):
        h = self.rows // self.sub
        return [(q * h, h) for q in range(self.sub)]

    def first(self):
        zt = up(self.z, Z // 2)
        self.shared(zt)
        for q, (lo, n) in enumerate(self.cut):
            side = 0 if q < len(self.cut) // 2 else 1
            part = self.mine(zt, lo, n)
            part[...] = part[...] + self.near[zt, pl.ds(lo, n), :]
            self.push(part, side, 0, q, lo, n)

    def push(self, part, side, step, q, lo, n):
        slot = side * 8 + step
        send(
            part,
            self.far.at[slot, pl.ds(lo, n), :],
            self.sems[2],
            self.sems[3].at[slot * len(self.cut) + q],
            (up(self.z, 1 - 2 * side) * CORES + self.c, self.b),
        )

    def pull(self, side, step, q, lo, n):
        slot = side * 8 + step
        arrived(self.far.at[slot, pl.ds(lo, n), :], self.sems[3].at[slot * len(self.cut) + q])
        return self.far[slot, pl.ds(lo, n), :]

    def second(self):
        for side in (0, 1):
            zt = up(self.z, (1 - 2 * side) * 7)
            self.shared(zt)
        half = len(self.cut) // 2
        for side in (0, 1):
            zt = up(self.z, (1 - 2 * side) * 7)
            for q, (lo, n) in enumerate(self.cut):
                if (q < half) != (side == 0):
                    part = self.mine(zt, lo, n)
                    part[...] = part[...] + self.near[zt, pl.ds(lo, n), :]
                    if self.sub > 1:
                        self.push(part, side, 1, q, lo, n)
        for q, (lo, n) in enumerate(self.cut):
            side = 0 if q < half else 1
            zt = up(self.z, (1 - 2 * side) * 7)
            part = self.mine(zt, lo, n)
            got = self.pull(side, 0, q, lo, n)
            part[...] = part[...] + (self.near[zt, pl.ds(lo, n), :] + got)
            if self.sub > 1:
                self.push(part, side, 1, q, lo, n)
        if self.sub == 1:
            for side in (0, 1):
                zt = up(self.z, (1 - 2 * side) * 7)
                self.push(self.mine(zt, 0, self.rows), side, 1, 0, 0, self.rows)

    def rest(self):
        def step(s, carry):
            for side in (0, 1):
                self.shared(lax.rem(self.z + (1 - 2 * side) * (8 - s) + Z, Z))
            for q, (lo, n) in enumerate(self.pieces()):
                for side in (0, 1):
                    zt = lax.rem(self.z + (1 - 2 * side) * (8 - s) + Z, Z)
                    part = self.mine(zt, lo, n)
                    got = self.pull(side, s - 1, q, lo, n)
                    part[...] = part[...] + (self.near[zt, pl.ds(lo, n), :] + got)
                    self.push(part, side, s, q, lo, n)
            return carry

        lax.fori_loop(2, 8, step, 0)
        self.shared(self.z)

    def total(self, q, lo, n):
        own = self.mine(self.z, lo, n)[...] + self.near[self.z, pl.ds(lo, n), :]
        return own + (self.pull(0, 7, q, lo, n) + self.pull(1, 7, q, lo, n))

    def drain(self):
        arrived(self.near, self.sems[0])
        arrived(self.far.at[pl.ds(0, 15)], self.sems[2])


class Fold:
    def __init__(self, buf, near, far, sib_send, sib_recv, ssem, rsem):
        self.buf, self.near, self.far = buf, near, far
        self.sems = sib_send, sib_recv, ssem, rsem
        self.d, self.b, self.z, self.c = place()

    def share(self, zt):
        start = pl.multiple_of((zt * CORES + 1 - self.c) * PACK, 8)
        send(
            self.buf.at[pl.ds(start, PACK), :],
            self.near.at[zt],
            self.sems[0],
            self.sems[1].at[zt],
            (self.z * CORES + 1 - self.c, self.b),
        )

    def span(self, side, k):
        if k != 8:
            return 0, PACK
        return (0, HALF) if side > 0 else (HALF, PACK - HALF)

    def landing(self, side, k):
        slot = (0 if side > 0 else 8) + k - 1
        lo, n = self.span(side, k)
        return self.far.at[slot, pl.ds(lo, n), :], self.sems[3].at[slot]

    def collect(self, zt, takes):
        arrived(self.near.at[zt], self.sems[1].at[zt])
        part = self.buf.at[pl.ds(pl.multiple_of((zt * CORES + self.c) * PACK, 8), PACK), :]
        part[...] = part[...] + self.near[zt]
        for side, child in takes:
            ref, sem = self.landing(side, child)
            lo, n = self.span(side, child)
            arrived(ref, sem)
            rows = part.at[pl.ds(lo, n), :]
            rows[...] = rows[...] + ref[...]
        return part

    def push(self, part, side, k):
        ref, sem = self.landing(side, k)
        lo, n = self.span(side, k)
        to = up(self.z, side * (k - PARENT[k])) * CORES + self.c
        send(part.at[pl.ds(lo, n), :], ref, self.sems[2], sem, (to, self.b))

    def run(self):
        part = self.collect(up(self.z, 8), ())
        for side in (1, -1):
            self.push(part, side, 8)
        for k in (7, 5, 2, 6, 4, 1, 3):
            for side in (1, -1):
                part = self.collect(up(self.z, side * k), [(side, n) for n in TREE.get(k, ())])
                self.push(part, side, k)
        return self.collect(self.z, [(side, n) for n in TREE[0] for side in (1, -1)])[...]

    def drain(self):
        arrived(self.near, self.sems[0])
        arrived(self.far.at[pl.ds(0, 15)], self.sems[2])


class Spread:
    def __init__(self, buf, ssem, rsem):
        self.buf, self.ssem, self.rsem = buf, ssem, rsem
        self.d, self.b, _, _ = place()

    def block(self, h, u, v):
        u, v = (u, v) if h == 0 else (v, u)
        return up4(self.b // X, v) * X + up4(self.b % X, u)

    def part(self, h, u, v, half):
        lo, n = ((0, CUT), (CUT, COLS - CUT))[h]
        if half:
            lo, n = lo + (half - 1) * n // 2, n // 2
        return self.buf.at[self.block(h, u, v), pl.ds(lo, n), :]

    def sem(self, h, u, v, half):
        if half == 2:
            return self.rsem.at[h * 24 + 16 + (2 if v == 0 else u + 1 + (u > 0))]
        return self.rsem.at[h * 24 + (u + 1) * 4 + v + 1]

    def send(self, h, u, v, half, axis, step):
        to = (step, 0) if axis == 0 else (0, step)
        seen = [2 if n == -2 else n for n in (u - to[0], v - to[1])]
        ref = self.part(h, u, v, half)
        send(ref, ref, self.ssem, self.sem(h, *seen, half), (self.d, self.block(h, *to)))

    def take(self, h, u, v, half=0):
        arrived(self.part(h, u, v, half), self.sem(h, u, v, half))

    def moves(self, h, value):
        self.part(h, 0, 0, 0)[...] = value()
        for axis in (1, 0):
            for step in (1, -1):
                self.send(h, 0, 0, 0, axis, step)
        yield [(0, 0)]
        for u, half in ((-1, 1), (1, 2)):
            self.take(h, u, 0)
            self.send(h, u, 0, half, 0, -u)
            for step in (1, -1):
                self.send(h, u, 0, 0, 1, step)
        yield [(-1, 0), (1, 0)]
        for v, half in ((-1, 1), (1, 2)):
            self.take(h, 0, v)
            self.send(h, 0, v, half, 1, -v)
        for half in (1, 2):
            self.take(h, 2, 0, half)
        for step in (1, -1):
            self.send(h, 2, 0, 0, 1, step)
        yield [(0, -1), (0, 1), (2, 0)]
        for u in (-1, 1, 2):
            for v, half in ((-1, 1), (1, 2)):
                self.take(h, u, v)
                self.send(h, u, v, half, 1, -v)
            yield [(u, -1), (u, 1)]
        for u in (0, -1, 1, 2):
            for half in (1, 2):
                self.take(h, u, 2, half)
            yield [(u, 2)]

    def steps(self, value):
        came = [set(), set()]
        given = set()
        halves = self.moves(0, lambda: value(0)), self.moves(1, lambda: value(1))
        for first, second in zip(*halves):
            came[0].update(first)
            came[1].update((v, u) for u, v in second)
            now = [o for o in NEAR if o in came[0] & came[1] - given]
            given.update(now)
            yield [self.block(0, *o) for o in now]

    def drain(self):
        arrived(self.buf.at[pl.ds(0, NBLK - 1)], self.ssem)


class Plane:
    def __init__(self, buf, ssem, rsem):
        self.buf, self.ssem, self.rsem = buf, ssem, rsem
        self.d, self.b, _, _ = place()

    def block(self, u, v):
        return up4(self.b // X, v) * X + up4(self.b % X, u)

    def part(self, u, v):
        return self.buf.at[self.block(u, v)]

    def sem(self, u, v):
        return self.rsem.at[(v + 1) * X + u + 1]

    def start(self, value):
        mine = self.part(0, 0)
        mine[...] = value
        for u, v in NEAR[:0:-1]:
            back = [2 if n == 2 else -n for n in (u, v)]
            send(mine, mine, self.ssem, self.sem(*back), (self.d, self.block(u, v)))

    def take(self, u, v):
        if (u, v) != (0, 0):
            arrived(self.part(u, v), self.sem(u, v))
        return self.part(u, v)[...]

    def finish(self):
        for u, v in NEAR[1:]:
            arrived(self.part(u, v), self.sem(u, v))

    def product(self, halves):
        total = 0
        for at in range(0, NBLK, 2):
            pair = NEAR[at:at + 2]
            left = jnp.concatenate([self.take(u, v) for u, v in pair], axis=1)
            right = [halves[pl.ds(pl.multiple_of(self.block(u, v) * 128, 128), 128), :] for u, v in pair]
            total += dot(stack(left, 0), jnp.concatenate(right, axis=0))
        return merge(total)

    def drain(self):
        arrived(self.buf.at[pl.ds(0, NBLK - 1)], self.ssem)


class Line:
    def __init__(self, buf, ssem, rsem, share_ssem, share_rsem):
        self.buf, self.ssem, self.rsem = buf, ssem, rsem
        self.share_sems = share_ssem, share_rsem
        self.d, self.b, self.z, self.c = place()

    def part(self, side, k, child):
        dd = up(self.z, -side * k) * CORES + self.c
        lo, n = 0, LINE
        if child == 8:
            n = LINE // 2
            lo = 0 if side > 0 else n
        return self.buf.at[pl.ds(pl.multiple_of(dd * LINE + lo, 8), n), :]

    def sem(self, side, k):
        return self.rsem.at[(0 if side > 0 else 8) + k - 1]

    def emit(self, k, side):
        for child in RELAY.get(k, ()):
            v = self.part(side, k, child)
            to = up(self.z, side * (child - k)) * CORES + self.c
            send(v, v, self.ssem, self.sem(side, child), (to, self.b))

    def share(self, dz):
        dd = up(self.z, dz) * CORES + self.c
        v = self.buf.at[pl.ds(pl.multiple_of(dd * LINE, 8), LINE), :]
        stage = [any(dz in pair for pair in pairs) for pairs in SETS].index(True)
        sem = self.share_sems[1].at[stage]
        send(v, v, self.share_sems[0], sem, (self.z * CORES + 1 - self.c, self.b))

    def start(self, value):
        v = self.buf.at[pl.ds(pl.multiple_of(self.d * LINE, 8), LINE), :]
        v[...] = value
        for side in (1, -1):
            self.emit(0, side)
        self.share(0)

    def relay(self, stage):
        for k in STAGES[stage]:
            for side in (1, -1):
                arrived(self.part(side, k, k), self.sem(side, k))
                self.emit(k, side)
            self.share(k)
            if k != 8:
                self.share(-k)

    def part_product(self, stage, halves, left=None):
        pairs = SETS[stage]
        arrived(self.buf.at[pl.ds(0, 2 * LINE * len(pairs)), :], self.share_sems[1].at[stage])
        total = 0
        for pair in pairs:
            rows = [pl.ds(pl.multiple_of(up(self.z, k) * 128, 128), 128) for k in pair]
            right = [stack(self.buf[r, :], 1) for r in rows]
            for r, v in zip(rows, right):
                halves[r, :] = v
            if left is not None:
                total += dot(jnp.concatenate([left[:, r] for r in rows], axis=1), jnp.concatenate(right, axis=0))
        return total

    def drain(self):
        arrived(self.buf.at[pl.ds(0, 15 * LINE), :], self.ssem)
        arrived(self.buf.at[pl.ds(0, H // 2), :], self.share_sems[0])


def eye(rows, cols, row0, col0, value):
    r = lax.broadcasted_iota(jnp.int32, (rows, cols), 0) + row0
    c = lax.broadcasted_iota(jnp.int32, (rows, cols), 1) + col0
    return jnp.where(r == c, F32(value), F32(0))


def kernel(
    counts, partials, out, pin, pt, sb, rv, ft, pg, sg, rg, zb, xb, xg0, yt, zc, zd, xc, yc,
    in_s, sib_s, sib_r, ring_s, ring_r, field_s, field_r, gsib_s, gsib_r, fold_s, fold_r,
    plane_s, plane_r, line_s, line_r, lshare_s, lshare_r,
):
    d, b, z, c = place()
    greet()
    pair0 = up(z, Z // 2) // 2

    def load(j):
        at = pl.multiple_of(lax.rem(pair0 + j + 8, 8) * PAIR, 128)
        window = pl.ds(at, PAIR)
        return pltpu.make_async_copy(partials.at[0, :, window], pin.at[:, window], in_s.at[j + 3])

    turns = (0, -1, 1, -2, 2, -3, 3, 4)
    for j in turns:
        load(j).start()

    weight = counts[0].astype(F32)
    scaled_eye = (eye(128, 128, 0, 0, 1.0) * weight).astype(BF16)
    for j in turns:
        load(j).wait()
        pair = lax.rem(pair0 + j + 8, 8)
        for t in range(7):
            at = pl.multiple_of(pair * PAIR + t * 128, 128)
            pt[pl.ds(at, 128), :] = lax.dot_general(
                scaled_eye, pin[:, pl.ds(at, 128)], (((1,), (1,)), ((), ())), preferred_element_type=F32
            )
    met()
    used = []
    ring = Ring(
        pt, COLS, sb, rv, [(q * 32, 32) for q in range(7)], 7, sib_s, sib_r, ring_s, ring_r
    )
    used.append(ring)
    for j in turns:
        pair = lax.rem(pair0 + j + 8, 8)
        ring.share(pair * 2)
        ring.share(pair * 2 + 1)
    ring.first()
    ring.second()
    ring.rest()

    def summed(h):
        pieces = ((0, 1, 2, 3), (4, 5, 6))[h]
        return jnp.concatenate([ring.total(q, *ring.cut[q]) for q in pieces], axis=0)

    whole = Spread(ft, field_s.at[0], field_r.at[0])
    used.append(whole)
    came = whole.steps(summed)
    blocks = next(came)
    field = ft[b]

    sq = jnp.sum(jnp.sum(field * field, axis=0, keepdims=True), axis=1, keepdims=True)
    sq = jnp.broadcast_to(sq, (8, 128))

    def put(i, carry):
        pg[pl.ds(pl.multiple_of(i * PACK + LINE, 8), 8), :] = sq
        return carry

    fold = Fold(pg, sg, rg, gsib_s, gsib_r, fold_s, fold_r)
    used.append(fold)
    right = stack(field, 1)

    def gram(i):
        v = stack(ft[i], 1)
        both = lax.dot_general(v, right, (((0,), (0,)), ((), ())), preferred_element_type=F32)
        res = merge(both)
        at = pl.multiple_of(i * 2 * PACK, 8)
        pg[pl.ds(at, LINE), :] = res[:LINE]
        pg[pl.ds(pl.multiple_of(at + PACK, 8), LINE), :] = res[LINE:]
        fold.share(i)

    lax.fori_loop(0, NDP, put, 0)
    while blocks is not None:
        for i in blocks:
            gram(i)
        blocks = next(came, None)
    packed = fold.run()

    def line(i):
        one = Line(zb.at[i], line_s.at[i], line_r.at[i], lshare_s.at[i], lshare_r.at[i])
        used.append(one)
        return one

    def plane(i, buf):
        one = Plane(buf, plane_s.at[i], plane_r.at[i])
        used.append(one)
        return one

    def square(packed, zg, xg, beside=lambda stage: None):
        zg.start(packed[:LINE])
        xg.start(packed)
        beside(0)
        zg.relay(0)
        beside(1)
        zg.relay(1)
        beside(2)
        xg.finish()
        inv = F32(1)
        if packed.shape[0] > LINE:
            total = sum(xg.buf[i, LINE:LINE + 1, :] for i in range(NBLK))
            inv = 1.0 / (jnp.sqrt(total[0, 0]) + EPS)
        xc[...] = stack(flat(xg.buf)[:LINE] * (inv * inv), 0)
        both = zg.part_product(0, zc, xc)
        zg.relay(2)
        beside(3)
        both += zg.part_product(1, zc, xc)
        both += zg.part_product(2, zc, xc)
        g = packed[:LINE] * (inv * inv)
        return inv, COEF_B * g + COEF_C * (merge(both) * (inv * inv)) + eye(LINE, 128, d * LINE, b * 128, COEF_A)

    def advance(packed, i, beside=lambda stage: None):
        zg = line(2 * i)
        inv, p = square(packed, zg, plane(3 * i, xg0 if i == 0 else xb.at[0]), beside)
        zp, xp, xu = line(2 * i + 1), plane(3 * i + 1, xb.at[1 + 2 * i]), plane(3 * i + 2, xb.at[2 + 2 * i])
        zp.start(p)
        xp.start(p)
        beside(4)
        zp.relay(0)
        xu.start(xp.product(zc) * (inv * inv))
        zp.relay(1)
        zp.part_product(0, zd)
        zp.relay(2)
        zp.part_product(1, zd)
        zp.part_product(2, zd)
        return inv, xu.product(zd)

    inv, g = advance(packed, 0)

    def apply(i, value):
        one = Spread(yt.at[i], field_s.at[i + 1], field_r.at[i + 1])
        used.append(one)
        moves = []

        def beside(stage):
            if stage == 0:
                v = value()
                moves.append(one.steps(lambda h: v[:CUT] if h == 0 else v[CUT:]))
            for _ in range((1, 1, 2, 2, 9)[stage]):
                next(moves[0], None)

        return beside

    first = apply(0, lambda: mm(flat(ft), zd))
    _, g = advance(g, 1, first)
    second = apply(1, lambda: mm(flat(yt.at[0]), zd) * (inv * GAIN))
    _, p = square(g, line(4), plane(6, xb.at[5]), second)
    zp = line(5)
    zp.start(p)
    second(4)
    yc[...] = stack(flat(yt.at[1]), 0)
    zp.relay(0)
    zp.relay(1)
    both = zp.part_product(0, zd, yc)
    zp.relay(2)
    both += zp.part_product(1, zd, yc)
    both += zp.part_product(2, zd, yc)
    out[...] = merge(both)
    for one in used:
        one.drain()


def body(partials, counts):
    vmem = pltpu.VMEM
    dma = pltpu.SemaphoreType.DMA
    out = pl.pallas_call(
        kernel,
        name="newton_schulz",
        out_shape=jax.ShapeDtypeStruct((COLS, ROWS), F32),
        in_specs=[
            pl.BlockSpec(memory_space=pltpu.SMEM),
            pl.BlockSpec(memory_space=pl.ANY),
        ],
        out_specs=pl.BlockSpec(memory_space=pltpu.VMEM),
        scratch_shapes=[
            vmem((ROWS, D), BF16),
            vmem((D, 128), F32),
            vmem((Z, COLS, 128), F32),
            vmem((16, COLS, 128), F32),
            vmem((NBLK, COLS, 128), F32),
            vmem((NDP * PACK, 128), F32),
            vmem((Z, PACK, 128), F32),
            vmem((16, PACK, 128), F32),
            vmem((6, H, 128), F32),
            vmem((6, NBLK, LINE, 128), F32),
            vmem((NBLK, PACK, 128), F32),
            vmem((2, NBLK, COLS, 128), F32),
            vmem((H, 256), BF16),
            vmem((H, 256), BF16),
            vmem((2 * LINE, H), BF16),
            vmem((2 * COLS, H), BF16),
            dma((8,)), dma, dma((Z,)), dma, dma((112,)),
            dma((3,)), dma((3, 48)),
            dma, dma((Z,)), dma, dma((16,)),
            dma((7,)), dma((7, 16)),
            dma((6,)), dma((6, 16)), dma((6,)), dma((6, 3)),
        ],
        compiler_params=pltpu.CompilerParams(
            collective_id=0, has_side_effects=True, vmem_limit_bytes=56 * 2**20
        ),
    )(counts, partials)
    return out.T


def solution(mesh):
    placed = (P("dp", "blk", None), P("dp"))
    return jax.shard_map(
        body, mesh=mesh, in_specs=placed, out_specs=P("blk", "dp"), check_vma=False
    )
```
